32 devices in a mesh: visit: 2 (over x), strip: 16 (over z, y, core).
Axes of the slice: x: 2, y: 2, z: 4, core: 2. Of those that a mesh axis runs over, the one named last changes fastest.
Arguments:
- template: bfloat16 [512, 1024], P('strip', 'visit'), may hold values from -60 to 60
- science_src: bfloat16 [2, 1024, 1024], P('visit', 'strip'), may hold values from -180 to 180
- target_rows: int32 [2, 1024], P('visit'), may hold values from 0 to 511, as said below
- row_taps: bfloat16 [45, 21], replicated, may hold values from -1.25 to 1.25
- col_taps: bfloat16 [45, 21], replicated, may hold values from -1.25 to 1.25
Outputs:
- difference: float32 [2, 512, 1024], P('visit', 'strip')
- kernel_coeffs: float32 [2, 45], P('visit')
The draws below stay inside these ranges and needn't reach their ends.
Inputs may be any that keep to these rules, and one draw needn't show every extreme that they name: `target_rows`: row j of a visit lies on strip device j // 64; its target's strip is target // 32. Of the 64 rows of one strip device at most 8 target the same strip, and in every visit one strip receives exactly 8 rows from every strip device.
All inputs are finite; a program needn't handle non-finite values.
Results may differ from the reference program's by a relative error of at most 0.0014.
Values may be sent and summed in bfloat16 or wider, within the bound.
A program may use at most 64 MiB of HBM per device.

```python
import math
import jax
import jax.numpy as jnp
from jax import lax

NBASIS = 45
TAPS = 21
ROWS_DEV = 32
COLS = 1024
SRC_DEV = 64
CAP = 8
VISITS = 2
NROWS = 512


def strip_routes(key):
    route_key = jax.random.fold_in(key, 11)
    sub_keys = jax.random.split(route_key, 4)
    strips = NROWS // ROWS_DEV
    others = (strips - 1) * CAP
    busiest = jax.random.randint(sub_keys[0], (VISITS, 1, 1), 0, strips)
    pick_keys = jax.random.split(sub_keys[1], VISITS * strips)
    chosen = jax.vmap(lambda k: jax.random.permutation(k, others)[:SRC_DEV - CAP])(pick_keys)
    chosen = chosen.reshape(VISITS, strips, SRC_DEV - CAP)
    spread_dest = chosen // CAP
    spread_dest = spread_dest + (spread_dest >= busiest).astype(jnp.int32)
    full_dest = jnp.broadcast_to(busiest, (VISITS, strips, CAP))
    listed = jnp.concatenate([full_dest, spread_dest], axis=2)
    mix_keys = jax.random.split(sub_keys[2], VISITS * strips)
    mixing = jax.vmap(lambda k: jax.random.permutation(k, SRC_DEV))(mix_keys).reshape(VISITS, strips, SRC_DEV)
    dest_strip = jnp.take_along_axis(listed, mixing, axis=2)
    row_pick = jax.random.randint(sub_keys[3], (VISITS, strips, SRC_DEV), 0, ROWS_DEV)
    return (dest_strip * ROWS_DEV + row_pick).reshape(VISITS, strips * SRC_DEV).astype(jnp.int32)


def template_field(key):
    sub_keys = jax.random.split(jax.random.fold_in(key, 23), 3)
    row_pos = jnp.arange(NROWS, dtype=jnp.float32) / NROWS
    trend = 0.6 + 0.8 * row_pos
    values = jnp.clip(jax.random.normal(sub_keys[0], (NROWS, COLS), jnp.float32), -4.0, 4.0)
    row_scale = jnp.exp(math.log(10.0) * (jax.random.uniform(sub_keys[1], (NROWS,), jnp.float32) - 0.5))
    col_scale = jnp.exp(math.log(10.0) * (jax.random.uniform(sub_keys[2], (COLS,), jnp.float32) - 0.5))
    return values * (trend * row_scale)[:, None] * col_scale[None, :]


def draw_template(key, part):
    return template_field(key).astype(jnp.bfloat16)


def draw_target_rows(key, part):
    return strip_routes(key)


def draw_science_src(key, part):
    field = template_field(key)
    targets = strip_routes(key)
    sub_keys = jax.random.split(jax.random.fold_in(key, 31), 2)
    visit_gain = jnp.exp(math.log(2.0) * jax.random.uniform(sub_keys[0], (VISITS, 1), jnp.float32, -1.0, 1.0))
    gain = (0.5 + targets.astype(jnp.float32) / NROWS) * visit_gain
    picked = field[targets]
    noise = 0.5 * jnp.clip(jax.random.normal(sub_keys[1], picked.shape, jnp.float32), -4.0, 4.0)
    return (gain[..., None] * picked + noise).astype(jnp.bfloat16)


def bell_draw(own_key, dims, deviation, most, kind=jnp.bfloat16):
    return jnp.clip(deviation * jax.random.normal(own_key, dims, jnp.float32), -most, most).astype(kind)


def setup_inputs(seed: int = 0) -> dict:
    key_of = jax.random.split(jax.random.key(seed), 6)
    template = draw_template(jax.random.fold_in(key_of[5], 71), 0)
    science_src = draw_science_src(jax.random.fold_in(key_of[5], 71), 0)
    target_rows = draw_target_rows(jax.random.fold_in(key_of[5], 71), 0)
    row_taps = bell_draw(key_of[3], (NBASIS, TAPS), TAPS ** -0.5, 1.25)
    col_taps = bell_draw(key_of[4], (NBASIS, TAPS), TAPS ** -0.5, 1.25)
    return dict(template=template, science_src=science_src, target_rows=target_rows, row_taps=row_taps, col_taps=col_taps)


PRECISE = lax.Precision.HIGHEST

def strip_basis(window, row_taps, col_taps):
    tap_count = col_taps.shape[1]
    out_width = window.shape[1] - tap_count + 1
    out_rows = window.shape[0] - tap_count + 1
    shifted = jnp.stack([window[:, t:t + out_width] for t in range(tap_count)]).astype(jnp.float32)
    smoothed = jnp.einsum('kt,thw->khw', col_taps.astype(jnp.float32), shifted, precision=PRECISE)
    smoothed = lax.optimization_barrier(smoothed.astype(jnp.bfloat16)).astype(jnp.float32)
    summed = jnp.zeros((row_taps.shape[0], out_rows, out_width), jnp.float32)
    for s in range(tap_count):
        summed = summed + row_taps[:, s].astype(jnp.float32)[:, None, None] * smoothed[:, s:s + out_rows, :]
    return summed.astype(jnp.bfloat16)

def solve_normal(gram_total, moment):
    factor = jnp.linalg.cholesky(gram_total)
    forward = lax.linalg.triangular_solve(factor, moment.T, left_side=True, lower=True)
    answer = lax.linalg.triangular_solve(factor, forward, left_side=True, lower=True, transpose_a=True)
    return answer.T

def reference(template, science_src, target_rows, row_taps, col_taps):
    margin = (row_taps.shape[1] - 1) // 2
    basis_count = row_taps.shape[0]
    science = jax.vmap(lambda source_rows, row_targets: jax.ops.segment_sum(source_rows.astype(jnp.float32), row_targets, num_segments=NROWS))(science_src, target_rows)
    framed = jnp.pad(template, ((margin, margin), (margin, margin)))
    strips = NROWS // ROWS_DEV

    def strip_images(index):
        window = lax.dynamic_slice_in_dim(framed, index * ROWS_DEV, ROWS_DEV + 2 * margin, 0)
        return strip_basis(window, row_taps, col_taps).astype(jnp.float32).reshape(basis_count, ROWS_DEV * COLS)

    def strip_science(index):
        return lax.dynamic_slice_in_dim(science, index * ROWS_DEV, ROWS_DEV, 1).reshape(VISITS, ROWS_DEV * COLS)

    def accumulate(running, index):
        gram_total, moment = running
        images = strip_images(index)
        gram_total = gram_total + jnp.dot(images, images.T, precision=PRECISE)
        moment = moment + jnp.einsum('kp,vp->vk', images, strip_science(index), precision=PRECISE)
        return ((gram_total, moment), None)
    start = (jnp.zeros((basis_count, basis_count), jnp.float32), jnp.zeros((VISITS, basis_count), jnp.float32))
    (gram_total, moment), _ = lax.scan(accumulate, start, jnp.arange(strips, dtype=jnp.int32))
    kernel_coeffs = solve_normal(gram_total, moment)

    def difference_rows(index):
        images = strip_images(index)
        model = jnp.einsum('vk,kp->vp', kernel_coeffs, images, precision=PRECISE)
        return (strip_science(index) - model).reshape(VISITS, ROWS_DEV, COLS)
    pieces = lax.map(difference_rows, jnp.arange(strips, dtype=jnp.int32))
    difference = jnp.transpose(pieces, (1, 0, 2, 3)).reshape(VISITS, NROWS, COLS)
    return (difference, kernel_coeffs)
```

```python
import functools
import math

import jax
import jax.numpy as jnp
from jax import lax
from jax.experimental import pallas as pl
from jax.experimental.pallas import tpu as pltpu
from jax.sharding import PartitionSpec as P

MESH = pl.DeviceIdType.MESH
F32 = jnp.float32
BF16 = jnp.bfloat16
LANES = 128
GROUP = 8
TILE = 16


def split_three(values):
    upper = values.astype(BF16).astype(F32)
    rest = values - upper
    middle = rest.astype(BF16).astype(F32)
    return upper, middle, rest - middle


def fit_kernel(
    dims,
    tmpl_ref, src_ref, place_ref, spread_ref, row_ref, col_ref,
    diff_ref, coef_ref,
    frame, outbox, inbox, wide, taps_pad, lag, band, rowband, sm, images, low_buf, high_buf,
    t_send, t_recv, s_send, s_recv, low_send, low_recv, high_send, high_recv,
):
    visits, strips, capacity, low, high = dims
    v = lax.axis_index("visit")
    me = lax.axis_index("strip")
    rows, width = tmpl_ref.shape
    cols = width * visits
    basis_count, taps = row_ref.shape
    margin = (taps - 1) // 2
    padded = images.shape[1]
    height = frame.shape[0]
    fold = TILE // capacity
    piece = cols // fold
    blocks = cols // LANES
    window = 2 * LANES
    lead = LANES // 2

    barrier = pltpu.get_barrier_semaphore()
    for off in range(1, strips):
        pl.semaphore_signal(
            barrier, inc=1, device_id=(v, lax.rem(me + off, strips)), device_id_type=MESH
        )
    for off in range(1, visits):
        other = lax.rem(v + off, visits)
        pl.semaphore_signal(barrier, inc=1, device_id=(other, me), device_id_type=MESH)

        @pl.when(me > 0)
        def _():
            pl.semaphore_signal(barrier, inc=1, device_id=(other, me - 1), device_id_type=MESH)

        @pl.when(me < strips - 1)
        def _():
            pl.semaphore_signal(barrier, inc=1, device_id=(other, me + 1), device_id_type=MESH)

    slot = lax.broadcasted_iota(jnp.int32, (strips * TILE, src_ref.shape[0]), 0)
    packed = jnp.zeros((strips * TILE, piece), F32)
    for f in range(fold):
        hit = (slot == place_ref[...] + f * capacity).astype(F32).astype(BF16)
        packed += jnp.dot(
            hit, src_ref[:, f * piece : (f + 1) * piece], preferred_element_type=F32
        )
    outbox[...] = packed.astype(BF16).reshape(strips, TILE, piece)

    neighbours = jnp.where(me > 0, 1, 0) + jnp.where(me < strips - 1, 1, 0)
    pl.semaphore_wait(barrier, strips - 1 + (visits - 1) * (1 + neighbours))

    def span(u):
        return pl.ds(pl.multiple_of(u * width, width), width)

    def main_copy(owner, to):
        return pltpu.make_async_remote_copy(
            src_ref=tmpl_ref, dst_ref=frame.at[pl.ds(TILE, rows), span(owner)],
            send_sem=t_send.at[0, to], recv_sem=t_recv.at[0, owner],
            device_id=(to, me), device_id_type=MESH,
        )

    def down_copy(owner, to, strip):
        return pltpu.make_async_remote_copy(
            src_ref=tmpl_ref.at[pl.ds(rows - TILE, TILE), :],
            dst_ref=frame.at[pl.ds(0, TILE), span(owner)],
            send_sem=t_send.at[1, to], recv_sem=t_recv.at[1, owner],
            device_id=(to, strip), device_id_type=MESH,
        )

    def up_copy(owner, to, strip):
        return pltpu.make_async_remote_copy(
            src_ref=tmpl_ref.at[pl.ds(0, TILE), :],
            dst_ref=frame.at[pl.ds(TILE + rows, TILE), span(owner)],
            send_sem=t_send.at[2, to], recv_sem=t_recv.at[2, owner],
            device_id=(to, strip), device_id_type=MESH,
        )

    for off in range(visits):
        to = lax.rem(v + off, visits)
        if off:
            main_copy(v, to).start()

        @pl.when(me < strips - 1)
        def _():
            down_copy(v, to, me + 1).start()

        @pl.when(me > 0)
        def _():
            up_copy(v, to, me - 1).start()

    def row_copy(off):
        to = lax.rem(me + off, strips)
        return pltpu.make_async_remote_copy(
            src_ref=outbox.at[to], dst_ref=inbox.at[me],
            send_sem=s_send.at[to], recv_sem=s_recv.at[me],
            device_id=(v, to), device_id_type=MESH,
        )

    for off in range(1, strips):
        row_copy(off).start()

    inbox[me] = outbox[me]
    frame[pl.ds(TILE, rows), span(v)] = tmpl_ref[...]

    @pl.when(me == 0)
    def _():
        frame[pl.ds(0, TILE), :] = jnp.zeros((TILE, cols), BF16)

    @pl.when(me == strips - 1)
    def _():
        frame[pl.ds(TILE + rows, TILE), :] = jnp.zeros((TILE, cols), BF16)

    shift = lead - margin
    taps_pad[...] = jnp.zeros(taps_pad.shape, F32)
    taps_pad[0, 0:basis_count, 0:taps] = col_ref[...].astype(F32)
    taps_pad[1, 0:basis_count, 0:taps] = row_ref[...].astype(F32)
    square = (LANES, LANES)
    turn = (
        lax.broadcasted_iota(jnp.int32, square, 0) + lax.broadcasted_iota(jnp.int32, square, 1)
        == LANES - shift
    ).astype(F32).astype(BF16)
    reverse = jnp.dot(taps_pad[0].astype(BF16), turn, preferred_element_type=F32)
    for j in range(TILE):
        lag[:, j, :] = pltpu.roll(reverse, j, 1) if j else reverse
    tile_row = lax.broadcasted_iota(jnp.int32, (TILE, LANES), 0)
    tile_col = lax.broadcasted_iota(jnp.int32, (TILE, LANES), 1)
    for i in range(window // TILE):
        gap = i * TILE + tile_row - tile_col - shift
        keep = (gap >= 0) & (gap < taps)
        turned = (i * TILE) % LANES
        for k in range(padded):
            entry = pltpu.roll(lag[k], turned, 1) if turned else lag[k]
            band[i * TILE : (i + 1) * TILE, k * LANES : (k + 1) * LANES] = jnp.where(
                keep, entry, 0.0
            ).astype(BF16)

    line = lax.broadcasted_iota(jnp.int32, (GROUP, LANES), 0)
    per_tile = LANES // height
    for g in range(padded // GROUP):
        base = pltpu.roll(taps_pad[1, g * GROUP : (g + 1) * GROUP, :], TILE - margin, 1)
        parts = []
        for q in range(GROUP // per_tile):
            part = jnp.zeros((GROUP, LANES), F32)
            for e in range(per_tile):
                moved = pltpu.roll(base, e * height, 1) if e else base
                part = jnp.where(line == q * per_tile + e, moved, part)
            parts.append(part)
        for r in range(0, rows, 2):
            pair = []
            for d in (r, r + 1):
                pair.append(
                    jnp.concatenate([pltpu.roll(p, d, 1) if d else p for p in parts], axis=1)
                )
            rowband[g, r * GROUP : (r + 2) * GROUP, :] = jnp.concatenate(pair, axis=0).astype(BF16)

    for off in range(1, visits):
        main_copy(lax.rem(v + off, visits), v).wait_recv()
    for off in range(visits):
        owner = lax.rem(v + off, visits)

        @pl.when(me > 0)
        def _():
            down_copy(owner, v, me).wait_recv()

        @pl.when(me < strips - 1)
        def _():
            up_copy(owner, v, me).wait_recv()

    full = jnp.concatenate(
        [frame[...].astype(F32), jnp.zeros((height, LANES), F32)], axis=1
    )
    shifted = pltpu.roll(full, lead, 1).astype(BF16)
    for b in range(blocks):
        wide[b * height : (b + 1) * height, :] = shifted[:, b * LANES : b * LANES + window]

    def group_image(g):
        span_g = GROUP * LANES
        out = jnp.dot(
            wide[...], band[:, g * span_g : (g + 1) * span_g], preferred_element_type=F32
        ).astype(BF16)
        for b in range(blocks):
            for k in range(GROUP):
                sm[g % 2, k * height : (k + 1) * height, b * LANES : (b + 1) * LANES] = out[
                    b * height : (b + 1) * height, k * LANES : (k + 1) * LANES
                ]
        return jnp.dot(rowband[g], sm[g % 2], preferred_element_type=F32)

    def put(pair, first, second):
        images[:, pair * TILE : (pair + 1) * TILE, :] = jnp.concatenate(
            [first.reshape(rows, GROUP, cols), second.reshape(rows, GROUP, cols)], axis=1
        ).astype(BF16)

    pairs = padded // TILE
    for pair in range(pairs - 1):
        put(pair, group_image(2 * pair), group_image(2 * pair + 1))
    first, second = group_image(2 * pairs - 2), group_image(2 * pairs - 1)

    for off in range(1, strips):
        source = lax.rem(me + off, strips)
        pltpu.make_async_remote_copy(
            src_ref=outbox.at[me], dst_ref=inbox.at[source],
            send_sem=s_send.at[me], recv_sem=s_recv.at[source],
            device_id=(v, source), device_id_type=MESH,
        ).wait_recv()
    arrived = inbox[...].reshape(strips * TILE, piece)
    spread = spread_ref[...]
    science = []
    for f in range(fold):
        mine = pltpu.roll(spread, f * capacity, 1) if f else spread
        science.append(jnp.dot(mine.astype(BF16), arrived, preferred_element_type=F32))
    science = jnp.concatenate(science, axis=1)
    upper, middle, lower = split_three(science)
    which = lax.broadcasted_iota(jnp.int32, science.shape, 0) % GROUP
    spare = basis_count % GROUP
    second = jnp.where(which == spare, upper, second)
    second = jnp.where(which == spare + 1, middle, second)
    second = jnp.where(which == spare + 2, lower, second)
    put(pairs - 1, first, second)

    def gram_step(r, total):
        image = images[r]
        return total + lax.dot_general(
            image, image, (((1,), (1,)), ((), ())), preferred_element_type=F32
        )

    gram = lax.fori_loop(0, rows, gram_step, jnp.zeros((padded, padded), F32), unroll=4)

    my_low = lax.rem(me, low)
    my_high = me // low
    low_buf[my_low] = jnp.zeros((padded, LANES), F32)
    low_buf[my_low, :, 0:padded] = gram

    def low_copy(slot_id, peer):
        return pltpu.make_async_remote_copy(
            src_ref=low_buf.at[slot_id], dst_ref=low_buf.at[slot_id],
            send_sem=low_send.at[peer], recv_sem=low_recv.at[slot_id],
            device_id=(v, my_high * low + peer), device_id_type=MESH,
        )

    def high_copy(slot_id, peer):
        return pltpu.make_async_remote_copy(
            src_ref=high_buf.at[slot_id], dst_ref=high_buf.at[slot_id],
            send_sem=high_send.at[peer], recv_sem=high_recv.at[slot_id],
            device_id=(v, peer * low + my_low), device_id_type=MESH,
        )

    for off in range(1, low):
        low_copy(my_low, lax.rem(my_low + off, low)).start()
    for off in range(1, low):
        peer = lax.rem(my_low + off, low)
        low_copy(peer, peer).wait_recv()
    high_buf[my_high] = jnp.sum(low_buf[...], axis=0)
    for off in range(1, high):
        high_copy(my_high, lax.rem(my_high + off, high)).start()
    for off in range(1, high):
        peer = lax.rem(my_high + off, high)
        high_copy(peer, peer).wait_recv()
    system = jnp.sum(high_buf[...], axis=0)

    rhs = basis_count
    lane = lax.broadcasted_iota(jnp.int32, (padded, LANES), 1)
    sub = lax.broadcasted_iota(jnp.int32, (padded, LANES), 0)
    moment = (
        system[:, rhs : rhs + 1] + system[:, rhs + 1 : rhs + 2] + system[:, rhs + 2 : rhs + 3]
    )
    system = jnp.where(lane == rhs, moment, system)
    for j in range(basis_count):
        pivot = system[j : j + 1, :] / system[j : j + 1, j : j + 1]
        column = jnp.where(sub == j, 0.0, system[:, j : j + 1])
        system = jnp.where(sub == j, pivot, system - column * pivot)
    answer = jnp.where((sub == lane) & (sub < basis_count), system[:, rhs : rhs + 1], 0.0)
    answer = jnp.sum(answer, axis=0, keepdims=True)
    coef_ref[...] = answer[:, 0:basis_count]

    upper, middle, lower = split_three(-answer)
    lane8 = lax.broadcasted_iota(jnp.int32, (GROUP, LANES), 1)
    upper = jnp.where((lane8[0:1] >= rhs) & (lane8[0:1] < rhs + 3), 1.0, upper)
    weights = jnp.where(line == 0, upper, jnp.where(line == 1, middle, jnp.where(line == 2, lower, 0.0)))
    weights = weights[:, 0:padded].astype(BF16)
    for r in range(rows):
        model = jnp.dot(weights, images[r], preferred_element_type=F32)
        diff_ref[r : r + 1, :] = jnp.sum(model, axis=0, keepdims=True)

    for off in range(visits):
        to = lax.rem(v + off, visits)
        if off:
            main_copy(v, to).wait_send()

        @pl.when(me < strips - 1)
        def _():
            down_copy(v, to, me + 1).wait_send()

        @pl.when(me > 0)
        def _():
            up_copy(v, to, me - 1).wait_send()

    for off in range(1, strips):
        row_copy(off).wait_send()
    for off in range(1, low):
        low_copy(my_low, lax.rem(my_low + off, low)).wait_send()
    for off in range(1, high):
        high_copy(my_high, lax.rem(my_high + off, high)).wait_send()


def body(template, science_src, target_rows, row_taps, col_taps):
    basis_count = row_taps.shape[0]
    strips = lax.axis_size("strip")
    visits = lax.axis_size("visit")
    rows_dev, part_width = template.shape
    full_width = part_width * visits
    src_dev = science_src.shape[1]
    capacity = max(2, 2 * src_dev // strips)
    fold = TILE // capacity
    piece = full_width // fold
    padded = (basis_count + 3 + TILE - 1) // TILE * TILE
    height = rows_dev + 2 * TILE
    low = 2 ** (int(math.log2(strips)) // 2)
    high = strips // low
    my_strip = lax.axis_index("strip")
    targets = target_rows[0].reshape(strips, src_dev)
    dest_strip = targets // rows_dev
    row_order = jnp.arange(src_dev, dtype=jnp.int32)
    shared_dest = (dest_strip[:, :, None] == dest_strip[:, None, :]) & (
        row_order[:, None] < row_order[None, :]
    )[None]
    arrival = jnp.sum(shared_dest.astype(jnp.int32), axis=1)
    place = lax.dynamic_slice_in_dim(dest_strip * TILE + arrival, my_strip, 1, 0)
    slot_ids = jnp.arange(strips * TILE, dtype=jnp.int32)
    anchor = (jnp.arange(strips, dtype=jnp.int32) * TILE)[:, None] + arrival
    aimed_here = dest_strip == my_strip
    local_row = targets - my_strip * rows_dev
    slot_hit = (aimed_here[..., None] & (anchor[..., None] == slot_ids)).reshape(
        strips * src_dev, strips * TILE
    )
    line_rows = jnp.arange(rows_dev * GROUP, dtype=jnp.int32) // GROUP
    row_hit = (local_row[..., None] == line_rows).reshape(strips * src_dev, rows_dev * GROUP)
    spread = lax.dot_general(
        row_hit.astype(BF16), slot_hit.astype(BF16), (((0,), (0,)), ((), ())),
        preferred_element_type=F32,
    )
    vmem = pl.BlockSpec(memory_space=pltpu.VMEM)
    dma = pltpu.SemaphoreType.DMA
    difference, coeffs = pl.pallas_call(
        functools.partial(fit_kernel, (visits, strips, capacity, low, high)),
        out_shape=(
            jax.ShapeDtypeStruct((rows_dev, full_width), F32),
            jax.ShapeDtypeStruct((1, basis_count), F32),
        ),
        in_specs=[vmem] * 6,
        out_specs=(vmem, vmem),
        scratch_shapes=[
            pltpu.VMEM((height, full_width), BF16),
            pltpu.VMEM((strips, TILE, piece), BF16),
            pltpu.VMEM((strips, TILE, piece), BF16),
            pltpu.VMEM((full_width // LANES * height, 2 * LANES), BF16),
            pltpu.VMEM((2, padded, LANES), F32),
            pltpu.VMEM((padded, TILE, LANES), F32),
            pltpu.VMEM((2 * LANES, padded * LANES), BF16),
            pltpu.VMEM((padded // GROUP, rows_dev * GROUP, GROUP * height), BF16),
            pltpu.VMEM((2, GROUP * height, full_width), BF16),
            pltpu.VMEM((rows_dev, padded, full_width), BF16),
            pltpu.VMEM((low, padded, LANES), F32),
            pltpu.VMEM((high, padded, LANES), F32),
            dma((3, visits)),
            dma((3, visits)),
            dma((strips,)),
            dma((strips,)),
            dma((low,)),
            dma((low,)),
            dma((high,)),
            dma((high,)),
        ],
        compiler_params=pltpu.CompilerParams(
            collective_id=0, has_side_effects=True, vmem_limit_bytes=50 * 1024 * 1024
        ),
    )(template, science_src[0], place, spread, row_taps, col_taps)
    return (difference[None], coeffs)


def solution(mesh):
    in_specs = (P("strip", "visit"), P("visit", "strip", None), P("visit", None), P(), P())
    out_specs = (P("visit", "strip", None), P("visit", None))
    return jax.shard_map(body, mesh=mesh, in_specs=in_specs, out_specs=out_specs, check_vma=False)
```

```python
import functools
import math

import jax
import jax.numpy as jnp
from jax import lax
from jax.experimental import pallas as pl
from jax.experimental.pallas import tpu as pltpu
from jax.sharding import PartitionSpec as P

MESH = pl.DeviceIdType.MESH
F32 = jnp.float32
BF16 = jnp.bfloat16
LANES = 128
GROUP = 8
TILE = 16


def split_three(values):
    upper = values.astype(BF16).astype(F32)
    rest = values - upper
    middle = rest.astype(BF16).astype(F32)
    return upper, middle, rest - middle


def fit_kernel(
    dims,
    tmpl_ref, src_ref, target_ref, row_ref, col_ref,
    diff_ref, coef_ref,
    frame, outbox, inbox, wide, taps_pad, lag, band, rowband, sm, images, science, low_buf, high_buf, rhs_buf,
    t_send, t_recv, s_send, s_recv, low_send, low_recv, high_send, high_recv,
    rhs_send, rhs_recv,
):
    visits, strips, capacity, low, high = dims
    v = lax.axis_index("visit")
    me = lax.axis_index("strip")
    rows, width = tmpl_ref.shape
    cols = width * visits
    basis_count, taps = row_ref.shape
    margin = (taps - 1) // 2
    padded = images.shape[1]
    height = frame.shape[0]
    fold = TILE // capacity
    piece = cols // fold
    blocks = cols // LANES
    window = 2 * LANES
    lead = LANES // 2

    barrier = pltpu.get_barrier_semaphore()
    for off in range(1, strips):
        pl.semaphore_signal(
            barrier, inc=1, device_id=(v, lax.rem(me + off, strips)), device_id_type=MESH
        )
    for off in range(1, visits):
        other = lax.rem(v + off, visits)
        pl.semaphore_signal(barrier, inc=1, device_id=(other, me), device_id_type=MESH)

        @pl.when(me > 0)
        def _():
            pl.semaphore_signal(barrier, inc=1, device_id=(other, me - 1), device_id_type=MESH)

        @pl.when(me < strips - 1)
        def _():
            pl.semaphore_signal(barrier, inc=1, device_id=(other, me + 1), device_id_type=MESH)

    src_dev = src_ref.shape[0]
    row_bits = int(math.log2(rows))
    earlier = (
        lax.broadcasted_iota(jnp.int32, (src_dev, src_dev), 0)
        < lax.broadcasted_iota(jnp.int32, (src_dev, src_dev), 1)
    ).astype(F32).astype(BF16)
    aim = lax.shift_right_logical(target_ref[pl.ds(me, 1), :], row_bits)
    hits = (lax.broadcasted_iota(jnp.int32, (strips, src_dev), 0) == aim).astype(F32)
    ahead = jnp.dot(hits.astype(BF16), earlier, preferred_element_type=F32)
    place = aim.astype(F32) * TILE + jnp.sum(hits * ahead, axis=0, keepdims=True)
    slot = lax.broadcasted_iota(jnp.int32, (strips * TILE, src_dev), 0).astype(F32)
    packed = jnp.zeros((strips * TILE, piece), F32)
    for f in range(fold):
        hit = (slot == place + float(f * capacity)).astype(F32).astype(BF16)
        packed += jnp.dot(
            hit, src_ref[:, f * piece : (f + 1) * piece], preferred_element_type=F32
        )
    outbox[...] = packed.astype(BF16).reshape(strips, TILE, piece)

    neighbours = jnp.where(me > 0, 1, 0) + jnp.where(me < strips - 1, 1, 0)
    pl.semaphore_wait(barrier, strips - 1 + (visits - 1) * (1 + neighbours))

    def span(u):
        return pl.ds(pl.multiple_of(u * width, width), width)

    def main_copy(owner, to):
        return pltpu.make_async_remote_copy(
            src_ref=tmpl_ref, dst_ref=frame.at[pl.ds(TILE, rows), span(owner)],
            send_sem=t_send.at[0, to], recv_sem=t_recv.at[0, owner],
            device_id=(to, me), device_id_type=MESH,
        )

    def down_copy(owner, to, strip):
        return pltpu.make_async_remote_copy(
            src_ref=tmpl_ref.at[pl.ds(rows - TILE, TILE), :],
            dst_ref=frame.at[pl.ds(0, TILE), span(owner)],
            send_sem=t_send.at[1, to], recv_sem=t_recv.at[1, owner],
            device_id=(to, strip), device_id_type=MESH,
        )

    def up_copy(owner, to, strip):
        return pltpu.make_async_remote_copy(
            src_ref=tmpl_ref.at[pl.ds(0, TILE), :],
            dst_ref=frame.at[pl.ds(TILE + rows, TILE), span(owner)],
            send_sem=t_send.at[2, to], recv_sem=t_recv.at[2, owner],
            device_id=(to, strip), device_id_type=MESH,
        )

    for off in range(visits):
        to = lax.rem(v + off, visits)
        if off:
            main_copy(v, to).start()

        @pl.when(me < strips - 1)
        def _():
            down_copy(v, to, me + 1).start()

        @pl.when(me > 0)
        def _():
            up_copy(v, to, me - 1).start()

    def partner(mask):
        to = me
        for bit in range(int(math.log2(strips))):
            if mask >> bit & 1:
                to = to + 2**bit * (1 - 2 * lax.rem(me // 2**bit, 2))
        return to

    def row_copy(mask):
        to = partner(mask)
        return pltpu.make_async_remote_copy(
            src_ref=outbox.at[to], dst_ref=inbox.at[me],
            send_sem=s_send.at[to], recv_sem=s_recv.at[me],
            device_id=(v, to), device_id_type=MESH,
        )

    for mask in range(strips - 1, 0, -1):
        row_copy(mask).start()

    inbox[me] = outbox[me]
    frame[pl.ds(TILE, rows), span(v)] = tmpl_ref[...]

    @pl.when(me == 0)
    def _():
        frame[pl.ds(0, TILE), :] = jnp.zeros((TILE, cols), BF16)

    @pl.when(me == strips - 1)
    def _():
        frame[pl.ds(TILE + rows, TILE), :] = jnp.zeros((TILE, cols), BF16)

    shift = lead - margin
    taps_pad[...] = jnp.zeros(taps_pad.shape, F32)
    taps_pad[0, 0:basis_count, 0:taps] = col_ref[...].astype(F32)
    taps_pad[1, 0:basis_count, 0:taps] = row_ref[...].astype(F32)
    square = (LANES, LANES)
    turn = (
        lax.broadcasted_iota(jnp.int32, square, 0) + lax.broadcasted_iota(jnp.int32, square, 1)
        == LANES - shift
    ).astype(F32).astype(BF16)
    reverse = jnp.dot(taps_pad[0].astype(BF16), turn, preferred_element_type=F32)
    for j in range(TILE):
        lag[:, j, :] = pltpu.roll(reverse, j, 1) if j else reverse
    tile_row = lax.broadcasted_iota(jnp.int32, (TILE, LANES), 0)
    tile_col = lax.broadcasted_iota(jnp.int32, (TILE, LANES), 1)
    for i in range(window // TILE):
        gap = i * TILE + tile_row - tile_col - shift
        keep = (gap >= 0) & (gap < taps)
        turned = (i * TILE) % LANES
        for k in range(padded):
            entry = pltpu.roll(lag[k], turned, 1) if turned else lag[k]
            band[i * TILE : (i + 1) * TILE, k * LANES : (k + 1) * LANES] = jnp.where(
                keep, entry, 0.0
            ).astype(BF16)

    line = lax.broadcasted_iota(jnp.int32, (GROUP, LANES), 0)
    per_tile = LANES // height
    for g in range(padded // GROUP):
        base = pltpu.roll(taps_pad[1, g * GROUP : (g + 1) * GROUP, :], TILE - margin, 1)
        parts = []
        for q in range(GROUP // per_tile):
            part = jnp.zeros((GROUP, LANES), F32)
            for e in range(per_tile):
                moved = pltpu.roll(base, e * height, 1) if e else base
                part = jnp.where(line == q * per_tile + e, moved, part)
            parts.append(part)
        for r in range(0, rows, 2):
            pair = []
            for d in (r, r + 1):
                pair.append(
                    jnp.concatenate([pltpu.roll(p, d, 1) if d else p for p in parts], axis=1)
                )
            rowband[g, r * GROUP : (r + 2) * GROUP, :] = jnp.concatenate(pair, axis=0).astype(BF16)

    targets = target_ref[...]
    mine = lax.shift_right_logical(targets, row_bits) == me
    order = jnp.dot(mine.astype(F32).astype(BF16), earlier, preferred_element_type=F32)
    order = jnp.where(mine, order, -1.0)
    goal = (targets - me * rows + 1).astype(F32)
    place3 = lax.broadcasted_iota(jnp.int32, (strips, TILE, src_dev), 1).astype(F32)
    line_row = (lax.broadcasted_iota(jnp.int32, (strips * TILE, rows * GROUP), 1) // GROUP).astype(F32)
    landing = []
    for f in range(fold):
        taken = (place3 - float(f * capacity)) == order[:, None, :]
        found = jnp.where(taken & (place3 >= float(f * capacity)), goal[:, None, :], 0.0)
        found = found.reshape(strips * TILE, src_dev)
        found = jnp.sum(found, axis=1, keepdims=True)
        landing.append((found == line_row + 1.0).astype(F32).astype(BF16))

    for off in range(1, visits):
        main_copy(lax.rem(v + off, visits), v).wait_recv()
    for off in range(visits):
        owner = lax.rem(v + off, visits)

        @pl.when(me > 0)
        def _():
            down_copy(owner, v, me).wait_recv()

        @pl.when(me < strips - 1)
        def _():
            up_copy(owner, v, me).wait_recv()

    full = jnp.concatenate(
        [frame[...].astype(F32), jnp.zeros((height, LANES), F32)], axis=1
    )
    shifted = pltpu.roll(full, lead, 1).astype(BF16)
    for b in range(blocks):
        wide[b * height : (b + 1) * height, :] = shifted[:, b * LANES : b * LANES + window]

    def group_image(g):
        span_g = GROUP * LANES
        out = jnp.dot(
            wide[...], band[:, g * span_g : (g + 1) * span_g], preferred_element_type=F32
        ).astype(BF16)
        for b in range(blocks):
            for k in range(GROUP):
                sm[g % 2, k * height : (k + 1) * height, b * LANES : (b + 1) * LANES] = out[
                    b * height : (b + 1) * height, k * LANES : (k + 1) * LANES
                ]
        return jnp.dot(rowband[g], sm[g % 2], preferred_element_type=F32)

    def put(pair, first, second):
        images[:, pair * TILE : (pair + 1) * TILE, :] = jnp.concatenate(
            [first.reshape(rows, GROUP, cols), second.reshape(rows, GROUP, cols)], axis=1
        ).astype(BF16)

    pairs = padded // TILE
    for pair in range(pairs):
        put(pair, group_image(2 * pair), group_image(2 * pair + 1))

    def gram_step(r, total):
        image = images[r]
        return total + lax.dot_general(
            image, image, (((1,), (1,)), ((), ())), preferred_element_type=F32
        )

    gram = lax.fori_loop(0, rows, gram_step, jnp.zeros((padded, padded), F32), unroll=4)

    my_low = lax.rem(me, low)
    my_high = me // low
    half = padded // 2
    low_buf[my_low] = jnp.zeros((half, LANES), F32)
    low_buf[my_low, :, 0:padded] = gram[0:half]
    low_buf[my_low, :, lead : lead + padded] = gram[half:padded]

    def low_copy(slot_id, peer):
        return pltpu.make_async_remote_copy(
            src_ref=low_buf.at[slot_id], dst_ref=low_buf.at[slot_id],
            send_sem=low_send.at[peer], recv_sem=low_recv.at[slot_id],
            device_id=(v, my_high * low + peer), device_id_type=MESH,
        )

    def high_copy(slot_id, peer):
        return pltpu.make_async_remote_copy(
            src_ref=high_buf.at[slot_id], dst_ref=high_buf.at[slot_id],
            send_sem=high_send.at[peer], recv_sem=high_recv.at[slot_id],
            device_id=(v, peer * low + my_low), device_id_type=MESH,
        )

    for off in range(1, low):
        low_copy(my_low, lax.rem(my_low + off, low)).start()
    for off in range(1, low):
        peer = lax.rem(my_low + off, low)
        low_copy(peer, peer).wait_recv()
    high_buf[my_high] = jnp.sum(low_buf[...], axis=0)
    for off in range(1, high):
        high_copy(my_high, lax.rem(my_high + off, high)).start()
    for mask in range(strips - 1, 0, -1):
        source = partner(mask)
        pltpu.make_async_remote_copy(
            src_ref=outbox.at[me], dst_ref=inbox.at[source],
            send_sem=s_send.at[me], recv_sem=s_recv.at[source],
            device_id=(v, source), device_id_type=MESH,
        ).wait_recv()
    arrived = inbox[...].reshape(strips * TILE, piece)
    for f in range(fold):
        science[:, :, f * piece : (f + 1) * piece] = lax.dot_general(
            landing[f], arrived, (((0,), (0,)), ((), ())), preferred_element_type=F32
        ).reshape(rows, GROUP, piece)

    bands = padded // GROUP

    def moment_step(r, total):
        for b in range(blocks):
            cells = images[r, :, b * LANES : (b + 1) * LANES].astype(F32)
            total = total + cells.reshape(bands, GROUP, LANES) * science[
                r, :, b * LANES : (b + 1) * LANES
            ][None]
        return total

    products = lax.fori_loop(0, rows, moment_step, jnp.zeros((bands, GROUP, LANES), F32), unroll=2)
    lane = lax.broadcasted_iota(jnp.int32, (padded, LANES), 1)
    sub = lax.broadcasted_iota(jnp.int32, (padded, LANES), 0)
    moment = jnp.sum(products.reshape(padded, LANES), axis=1, keepdims=True)
    moment = jnp.sum(jnp.where(sub == lane, moment, 0.0), axis=0, keepdims=True)
    rhs_buf[me] = jnp.where(line == 0, moment, 0.0)

    def rhs_copy(mask):
        to = partner(mask)
        return pltpu.make_async_remote_copy(
            src_ref=rhs_buf.at[me], dst_ref=rhs_buf.at[me],
            send_sem=rhs_send.at[to], recv_sem=rhs_recv.at[me],
            device_id=(v, to), device_id_type=MESH,
        )

    for mask in range(strips - 1, 0, -1):
        rhs_copy(mask).start()

    for off in range(1, high):
        peer = lax.rem(my_high + off, high)
        high_copy(peer, peer).wait_recv()
    halves = jnp.sum(high_buf[...], axis=0)

    system = jnp.concatenate([halves, pltpu.roll(halves, lead, 1)], axis=0)
    system = jnp.where(lane < lead, system, (lane - lead == sub).astype(F32))
    for j in range(basis_count):
        pivot = system[j : j + 1, :] / system[j : j + 1, j : j + 1]
        column = jnp.where(sub == j, 0.0, system[:, j : j + 1])
        system = jnp.where(sub == j, pivot, system - column * pivot)
    inverse = pltpu.roll(system, lead, 1)
    inverse = jnp.where((lane < basis_count) & (sub < basis_count), inverse, 0.0)

    for mask in range(strips - 1, 0, -1):
        source = partner(mask)
        pltpu.make_async_remote_copy(
            src_ref=rhs_buf.at[me], dst_ref=rhs_buf.at[source],
            send_sem=rhs_send.at[me], recv_sem=rhs_recv.at[source],
            device_id=(v, source), device_id_type=MESH,
        ).wait_recv()
    moment = jnp.sum(jnp.sum(rhs_buf[...], axis=0), axis=0, keepdims=True)
    answer = jnp.sum(inverse * moment, axis=1, keepdims=True)
    answer = jnp.sum(jnp.where(sub == lane, answer, 0.0), axis=0, keepdims=True)
    coef_ref[...] = answer[:, 0:basis_count]

    upper, middle, lower = split_three(-answer)
    weights = jnp.where(line == 0, upper, jnp.where(line == 1, middle, jnp.where(line == 2, lower, 0.0)))
    weights = weights[:, 0:padded].astype(BF16)
    for r in range(rows):
        model = jnp.dot(weights, images[r], preferred_element_type=F32)
        diff_ref[r : r + 1, :] = science[r, 0:1, :] + jnp.sum(model, axis=0, keepdims=True)

    for off in range(visits):
        to = lax.rem(v + off, visits)
        if off:
            main_copy(v, to).wait_send()

        @pl.when(me < strips - 1)
        def _():
            down_copy(v, to, me + 1).wait_send()

        @pl.when(me > 0)
        def _():
            up_copy(v, to, me - 1).wait_send()

    for mask in range(strips - 1, 0, -1):
        row_copy(mask).wait_send()
        rhs_copy(mask).wait_send()
    for off in range(1, low):
        low_copy(my_low, lax.rem(my_low + off, low)).wait_send()
    for off in range(1, high):
        high_copy(my_high, lax.rem(my_high + off, high)).wait_send()


def body(template, science_src, target_rows, row_taps, col_taps):
    basis_count = row_taps.shape[0]
    strips = lax.axis_size("strip")
    visits = lax.axis_size("visit")
    rows_dev, part_width = template.shape
    full_width = part_width * visits
    src_dev = science_src.shape[1]
    capacity = max(2, 2 * src_dev // strips)
    fold = TILE // capacity
    piece = full_width // fold
    padded = (basis_count + TILE - 1) // TILE * TILE
    height = rows_dev + 2 * TILE
    low = 2 ** (int(math.log2(strips)) // 2)
    high = strips // low
    targets = target_rows[0].reshape(strips, src_dev)
    vmem = pl.BlockSpec(memory_space=pltpu.VMEM)
    dma = pltpu.SemaphoreType.DMA
    difference, coeffs = pl.pallas_call(
        functools.partial(fit_kernel, (visits, strips, capacity, low, high)),
        out_shape=(
            jax.ShapeDtypeStruct((rows_dev, full_width), F32),
            jax.ShapeDtypeStruct((1, basis_count), F32),
        ),
        in_specs=[vmem] * 5,
        out_specs=(vmem, vmem),
        scratch_shapes=[
            pltpu.VMEM((height, full_width), BF16),
            pltpu.VMEM((strips, TILE, piece), BF16),
            pltpu.VMEM((strips, TILE, piece), BF16),
            pltpu.VMEM((full_width // LANES * height, 2 * LANES), BF16),
            pltpu.VMEM((2, padded, LANES), F32),
            pltpu.VMEM((padded, TILE, LANES), F32),
            pltpu.VMEM((2 * LANES, padded * LANES), BF16),
            pltpu.VMEM((padded // GROUP, rows_dev * GROUP, GROUP * height), BF16),
            pltpu.VMEM((2, GROUP * height, full_width), BF16),
            pltpu.VMEM((rows_dev, padded, full_width), BF16),
            pltpu.VMEM((rows_dev, GROUP, full_width), F32),
            pltpu.VMEM((low, padded // 2, LANES), F32),
            pltpu.VMEM((high, padded // 2, LANES), F32),
            pltpu.VMEM((strips, GROUP, LANES), F32),
            dma((3, visits)),
            dma((3, visits)),
            dma((strips,)),
            dma((strips,)),
            dma((low,)),
            dma((low,)),
            dma((high,)),
            dma((high,)),
            dma((strips,)),
            dma((strips,)),
        ],
        compiler_params=pltpu.CompilerParams(
            collective_id=0, has_side_effects=True, vmem_limit_bytes=50 * 1024 * 1024
        ),
    )(template, science_src[0], targets, row_taps, col_taps)
    return (difference[None], coeffs)


def solution(mesh):
    in_specs = (P("strip", "visit"), P("visit", "strip", None), P("visit", None), P(), P())
    out_specs = (P("visit", "strip", None), P("visit", None))
    return jax.shard_map(body, mesh=mesh, in_specs=in_specs, out_specs=out_specs, check_vma=False)
```
